32 devices in a mesh: dp: 2 (over x), context: 4 (over y, core), tensor: 4 (over z).
Axes of the slice: x: 2, y: 2, z: 4, core: 2. Of those that a mesh axis runs over, the one named last changes fastest.
Arguments:
- tokens: bfloat16 [8192, 4096], P(('dp', 'context'), 'tensor'), parts along dimension 0, may hold values from -6 to 6
- norm_gain: float32 [4096], replicated, may hold values from 0.5 to 1.5
- in_weight: bfloat16 [3, 4096, 4096], P(None, 'context', 'tensor'), may hold values from -0.09375 to 0.09375
- short_taps: float32 [3, 7, 4096], P(None, None, 'tensor'), may hold values from -2.5 to 2.5
- long_filter: float32 [4096, 128], P('tensor'), may hold values from -0.5 to 0.5
- skip_bias: float32 [4096], P('tensor'), may hold values from -3 to 3
- segment_ids: int32 [8192], P('dp'), parts along dimension 0, may hold values from 0 to 31, never falling along the last dimension, each value on 1 to 256 neighbouring positions
Outputs:
- mixed: bfloat16 [8192, 4096], P(('dp', 'context'), 'tensor'), parts along dimension 0
The draws below stay inside these ranges and needn't reach their ends.
There are 2 independent parts, one for each index of `dp`. The reference program is written for one: setup_inputs(seed, part) draws one part's arguments, and reference() takes and returns one part's arrays. A program takes and returns all parts, laid end to end along the dimension named above; an argument that names none is the same for every part. Nothing has to cross between parts.
Inputs may be any that keep to these rules, and one draw needn't show every extreme that they name: `segment_ids`: never falling, starting at 0; every document has 1 to 256 tokens and some has exactly 256.
All inputs are finite; a program needn't handle non-finite values.
Results may differ from the reference program's by a relative error of at most 0.0086.
Values may be sent and summed in bfloat16 or wider, within the bound.
A program may use at most 128 MiB of HBM per device.

```python
import math
import jax
import jax.numpy as jnp
import numpy as np
from jax import lax

DIN = 4096
CHANNELS = 4096
FILT = 128
TAPS = 7
SEQ = 4096


def level_of(rng, extent, pieces, least, high):
    def one(dim, blocks):
        draws = jax.random.uniform(jax.random.fold_in(jax.random.fold_in(rng, 6), dim), (blocks,), jnp.float32, least / len(pieces), high / len(pieces))
        return jnp.repeat(jnp.exp(draws), extent[dim] // blocks).reshape((-1,) + (1,) * (len(extent) - dim - 1))

    gain = one(*pieces[0])
    for cut in pieces[1:]:
        gain = gain * one(*cut)
    return gain


def split_up(number_of, total, bound, skew):
    loads = [(1 << 20) // math.isqrt(grade ** skew) + 1 for grade in range(2, number_of + 1)]
    surplus, holding = total - bound - (number_of - 1), [1] * (number_of - 1)
    while surplus > 0:
        candidates = [i for i in range(number_of - 1) if holding[i] < bound]
        pool, budget = sum([loads[i] for i in candidates]), surplus
        for i in candidates:
            addition = min(bound - holding[i], max(1, budget * loads[i] // pool), surplus)
            holding[i] = holding[i] + addition
            surplus = surplus - addition
    return np.array([bound] + holding)


def ragged_sizes(stream_key, number_of, total, bound, lean):
    if number_of == 2:
        one = jax.random.randint(stream_key, (), max(1, total - bound), min(bound, total - 1) + 1)
        return jnp.stack([one, total - one])
    sizes = jnp.asarray(split_up(number_of, total, bound, lean), jnp.int32)
    couples = (number_of - 1) // 2
    source_of, taker = sizes[1:1 + 2 * couples:2], sizes[2:2 + 2 * couples:2]
    margin = jnp.minimum(source_of - 1, bound - taker)
    passed = jax.random.randint(jax.random.fold_in(stream_key, 1), (couples,), 0, 1 << 20) % (margin + 1)
    sizes = sizes.at[1:1 + 2 * couples:2].set(source_of - passed).at[2:2 + 2 * couples:2].set(taker + passed)
    return sizes[jax.random.permutation(jax.random.fold_in(stream_key, 2), number_of)]


def normal_values(stream_key, extent, deviation, most, split=(), kind=jnp.bfloat16):
    level = level_of(stream_key, extent, split, -0.22, 0.18) if split else 1.0
    array = jax.random.normal(stream_key, extent, jnp.float32) * deviation * level
    return jnp.minimum(jnp.maximum(array, -most), most).astype(kind)


def setup_inputs(seed: int = 0, part: int = 0) -> dict:
    streams_of = jax.random.split(jax.random.key(seed), 8)
    own_keys = jax.random.split(jax.random.fold_in(streams_of[7], part), 8)
    return {
        "tokens": normal_values(own_keys[0], (SEQ, DIN), 1.0, 6.0, ((0, 4), (1, 4))),
        "norm_gain": jnp.clip(1.0 + 0.1 * jax.random.normal(streams_of[1], (DIN,), jnp.float32), 0.5, 1.5),
        "in_weight": normal_values(streams_of[2], (3, DIN, CHANNELS), DIN ** -0.5, 0.09375, ((1, 4), (2, 4))),
        "short_taps": normal_values(streams_of[3], (3, TAPS, CHANNELS), 0.4, 2.5, ((2, 4),), jnp.float32),
        "long_filter": normal_values(streams_of[4], (CHANNELS, FILT), 0.09, 0.5, ((0, 4),), jnp.float32),
        "skip_bias": normal_values(streams_of[5], (CHANNELS,), 0.5, 3.0, ((0, 4),), jnp.float32),
        "segment_ids": jnp.searchsorted(jnp.cumsum(ragged_sizes(own_keys[6], SEQ // 128, SEQ, 256, 0)), jnp.arange(SEQ), side="right").astype(jnp.int32),
    }


def distances(segment_ids):
    count = segment_ids.shape[0]
    places = jnp.arange(count, dtype=jnp.int32)
    earlier = jnp.concatenate([segment_ids[:1] - 1, segment_ids[:-1]])
    starts = jnp.where(segment_ids != earlier, places, jnp.zeros_like(places))
    first = lax.cummax(starts, axis=0)
    return (places - first).astype(jnp.int32)

def reference(tokens, norm_gain, in_weight, short_taps, long_filter, skip_bias, segment_ids):
    dist = distances(segment_ids)
    wide = tokens.astype(jnp.float32)
    scale = lax.rsqrt(lax.optimization_barrier(jnp.mean(wide * wide, axis=1, keepdims=True)) + 1e-06)
    normed = (wide * scale * norm_gain[None, :]).astype(jnp.bfloat16)
    proj = jnp.stack([jnp.dot(normed, in_weight[g], preferred_element_type=jnp.float32) for g in range(3)]).astype(jnp.bfloat16)
    seq = tokens.shape[0]
    lead = TAPS - 1
    padded = jnp.concatenate([jnp.zeros((3, lead, proj.shape[2]), jnp.bfloat16), proj], axis=1)
    feat = jnp.zeros(proj.shape, jnp.float32)
    for lag in range(TAPS):
        shifted = padded[:, lead - lag:lead - lag + seq].astype(jnp.float32)
        valid = (dist >= lag).astype(jnp.float32)
        feat = feat + short_taps[:, lag][:, None, :] * shifted * valid[None, :, None]
    inner = (feat[1] * feat[2]).astype(jnp.bfloat16)
    inner_wide = inner.astype(jnp.float32)
    zpad = jnp.concatenate([jnp.zeros((FILT - 1, inner.shape[1]), jnp.float32), inner_wide], axis=0)
    filt = jnp.transpose(long_filter)

    def turn(lag, acc):
        source = lax.dynamic_slice_in_dim(zpad, (FILT - 1 - lag).astype(jnp.int32), seq, 0)
        weight = lax.dynamic_slice_in_dim(filt, lag.astype(jnp.int32), 1, 0)
        valid = (dist >= lag).astype(jnp.float32)
        return acc + weight * source * valid[:, None]
    conv = lax.fori_loop(0, FILT, turn, jnp.zeros(inner.shape, jnp.float32))
    return (feat[0] * (conv + skip_bias[None, :] * inner_wide)).astype(jnp.bfloat16)
```

```python
import functools
import math

import jax
import jax.numpy as jnp
import numpy as np
from jax import lax
from jax.experimental import pallas as pl
from jax.experimental.pallas import tpu as pltpu
from jax.sharding import PartitionSpec as P

MESH = pl.DeviceIdType.MESH
PIECES = 8
HALO = 144
BLOCK = 128
POINTS = 256


def gather_kernel(nt, nc, x_in, w_in, gain, out, xbuf, wbuf, normed, loc, xs, xr, ys, yr, ps, pr, cs, cr, os_, or_, hs, hr):
    d = lax.axis_index("dp")
    i = lax.axis_index("context")
    t = lax.axis_index("tensor")
    y, c = i // 2, i % 2
    ny = nc // 2
    rows = x_in.shape[0] // PIECES
    deep = w_in.shape[1]
    half = deep // 2
    sib = (d, i + 1 - 2 * c, t)
    peer = (1 - d, i, t)

    mine_x = pltpu.make_async_copy(x_in, xbuf.at[t], loc.at[0])
    mine_w = pltpu.make_async_copy(w_in, wbuf.at[:, pl.ds(i * deep, deep), :], loc.at[1])
    mine_x.start()
    mine_w.start()

    bar = pltpu.get_barrier_semaphore()

    def greet(dev):
        pl.semaphore_signal(bar, inc=1, device_id=dev, device_id_type=MESH)

    greet(sib)
    greet(peer)
    peers = jnp.int32(2)
    for cond, dev in (
        (t > 0, (d, i, t - 1)),
        (t < nt - 1, (d, i, t + 1)),
        (y > 0, (d, i - 2, t)),
        (y < ny - 1, (d, i + 2, t)),
        ((c == 0) & (i > 0), (d, i - 1, t)),
        ((c == 1) & (i < nc - 1), (d, i + 1, t)),
    ):
        peers = peers + cond.astype(jnp.int32)

        @pl.when(cond)
        def _():
            greet(dev)

    pl.semaphore_wait(bar, peers)

    def spot(r):
        return pl.multiple_of(lax.rem(r + PIECES - 2, PIECES) * rows, rows)

    def xcopy(side, hop, r, block, first):
        place = pl.ds(spot(r), rows)
        dst = xbuf.at[block, place, :]
        src = x_in.at[place, :] if first else dst
        to = (d, i, t + 1) if side == 0 else (d, i, t - 1)
        return pltpu.make_async_remote_copy(src, dst, xs.at[side, hop, r], xr.at[side, hop, r], device_id=to, device_id_type=MESH)

    def x_sends(side, hop):
        return (t < nt - 1) & (t - hop >= 0) if side == 0 else (t > 0) & (t + hop < nt)

    def x_takes(side, hop):
        return t - 1 - hop >= 0 if side == 0 else t + 1 + hop < nt

    def x_sent(side, hop):
        return t - hop if side == 0 else t + hop

    def x_taken(side, hop):
        return t - 1 - hop if side == 0 else t + 1 + hop

    def when(cond, f):
        pl.when(cond)(f)

    def wspan(block, part):
        return pl.ds(pl.multiple_of(block * deep + part * half, half), half)

    def ycopy(side, hop, g, yb, first):
        place = wspan(yb * 2 + c, d)
        dst = wbuf.at[g, place, :]
        src = w_in.at[g, pl.ds(pl.multiple_of(d * half, half), half), :] if first else dst
        to = (d, i + 2, t) if side == 0 else (d, i - 2, t)
        return pltpu.make_async_remote_copy(src, dst, ys.at[side, hop, g], yr.at[side, hop, g], device_id=to, device_id_type=MESH)

    def y_sends(side, hop):
        return (y < ny - 1) & (y - hop >= 0) if side == 0 else (y > 0) & (y + hop < ny)

    def y_takes(side, hop):
        return y - 1 - hop >= 0 if side == 0 else y + 1 + hop < ny

    def y_sent(side, hop):
        return y - hop if side == 0 else y + hop

    def y_taken(side, hop):
        return y - 1 - hop if side == 0 else y + 1 + hop

    def pcopy(side, hop, g, yb, part):
        at = wbuf.at[g, wspan(yb * 2 + c, part), :]
        return pltpu.make_async_remote_copy(at, at, ps.at[side, hop, g], pr.at[side, hop, g], device_id=peer, device_id_type=MESH)

    def ccopy(side, hop, g, via, yb, core, part):
        at = wbuf.at[g, wspan(yb * 2 + core, part), :]
        return pltpu.make_async_remote_copy(at, at, cs.at[side, hop, g, via], cr.at[side, hop, g, via], device_id=sib, device_id_type=MESH)

    def ocopy(block):
        at = wbuf.at[:, pl.ds(pl.multiple_of(block * deep, deep), deep), :]
        return pltpu.make_async_remote_copy(w_in, at, os_, or_, device_id=sib, device_id_type=MESH)

    sides = (0, 1)

    for g in range(3):
        for side in sides:
            when(y_sends(side, 0), lambda: ycopy(side, 0, g, y, True).start())

    def start_own(r, carry):
        for side in sides:
            when(x_sends(side, 0), lambda: xcopy(side, 0, r, t, True).start())
        return carry

    lax.fori_loop(0, PIECES, start_own, 0)
    ocopy(i).start()

    def pass_x(r, carry):
        for hop in range(nt - 2):
            for side in sides:
                @pl.when(x_takes(side, hop))
                def _():
                    xcopy(side, hop, r, x_taken(side, hop), False).wait_recv()

                when(x_sends(side, hop + 1), lambda: xcopy(side, hop + 1, r, x_sent(side, hop + 1), False).start())
        return carry

    def pass_w(g):
        for hop in range(ny - 1):
            for side in sides:
                @pl.when(y_takes(side, hop))
                def _():
                    yb = y_taken(side, hop)
                    ycopy(side, hop, g, yb, False).wait_recv()
                    pcopy(side, hop, g, yb, d).start()
                    ccopy(side, hop, g, 0, yb, c, d).start()

                if hop + 1 < ny - 1:
                    when(y_sends(side, hop + 1), lambda: ycopy(side, hop + 1, g, y_sent(side, hop + 1), False).start())

    def pass_p(g):
        for hop in range(ny - 1):
            for side in sides:
                @pl.when(y_takes(side, hop))
                def _():
                    yb = y_taken(side, hop)
                    pcopy(side, hop, g, yb, 1 - d).wait_recv()
                    ccopy(side, hop, g, 1, yb, c, 1 - d).start()

    cuts = (2, 4, 6)
    at = 0
    for g in range(3):
        lax.fori_loop(at, cuts[g], pass_x, 0)
        at = cuts[g]
        pass_w(g)
        if g:
            pass_p(g - 1)
    lax.fori_loop(at, PIECES, pass_x, 0)
    pass_p(2)

    mine_x.wait()
    mine_w.wait()
    ocopy(sib[1]).wait_recv()
    for g in range(3):
        for hop in range(ny - 1):
            for side in sides:
                @pl.when(y_takes(side, hop))
                def _():
                    yb = y_taken(side, hop)
                    ccopy(side, hop, g, 0, yb, 1 - c, d).wait_recv()
                    ccopy(side, hop, g, 1, yb, 1 - c, 1 - d).wait_recv()

    wide = w_in.shape[2]
    tile = min(512, wide)
    feats = x_in.shape[1]

    def project(r):
        for side in sides:
            when(x_takes(side, nt - 2), lambda: xcopy(side, nt - 2, r, x_taken(side, nt - 2), False).wait_recv())
        place = pl.ds(spot(r), rows)
        total = jnp.zeros((rows, 1), jnp.float32)
        for k in range(nt):
            v = xbuf[k, place, :].astype(jnp.float32)
            total = total + jnp.sum(v * v, axis=1, keepdims=True)
        scale = lax.rsqrt(total * (1.0 / (feats * nt)) + 1e-06)
        for k in range(nt):
            v = xbuf[k, place, :].astype(jnp.float32)
            cols = pl.ds(k * feats, feats)
            normed[:, cols] = (v * scale * gain[:, cols]).astype(jnp.bfloat16)
        to = pl.ds(pl.multiple_of(HALO + spot(r), 16), rows)

        def one(n, carry):
            g = n // (wide // tile)
            cols = pl.ds(pl.multiple_of((n % (wide // tile)) * tile, tile), tile)
            out[g, to, cols] = jnp.dot(normed[...], wbuf[g, :, cols], preferred_element_type=jnp.float32).astype(jnp.bfloat16)
            return carry

        lax.fori_loop(0, 3 * (wide // tile), one, 0)

    def project_step(r, carry):
        project(r)
        return carry

    total_rows = rows * PIECES

    def hcopy():
        return pltpu.make_async_remote_copy(
            out.at[:, pl.ds(total_rows, HALO), :], out.at[:, pl.ds(0, HALO), :], hs, hr, device_id=(d, i + 1, t), device_id_type=MESH
        )

    @pl.when(i == 0)
    def _():
        out[:, 0:HALO, :] = jnp.zeros((3, HALO, wide), jnp.bfloat16)

    lax.fori_loop(0, 2, project_step, 0)
    when(i < nc - 1, lambda: hcopy().start())
    lax.fori_loop(2, PIECES, project_step, 0)

    def drain(r, carry):
        for hop in range(nt - 1):
            for side in sides:
                when(x_sends(side, hop), lambda: xcopy(side, hop, r, x_sent(side, hop), False).wait_send())
        return carry

    lax.fori_loop(0, PIECES, drain, 0)
    for g in range(3):
        for hop in range(ny - 1):
            for side in sides:
                when(y_sends(side, hop), lambda: ycopy(side, hop, g, y_sent(side, hop), False).wait_send())

                @pl.when(y_takes(side, hop))
                def _():
                    yb = y_taken(side, hop)
                    pcopy(side, hop, g, yb, d).wait_send()
                    ccopy(side, hop, g, 0, yb, c, d).wait_send()
                    ccopy(side, hop, g, 1, yb, c, 1 - d).wait_send()
    ocopy(i).wait_send()
    when(i < nc - 1, lambda: hcopy().wait_send())
    when(i > 0, lambda: hcopy().wait_recv())


def project_all(nt, nc, tokens, in_weight, gain):
    rows, feats = tokens.shape
    deep, wide = in_weight.shape[1:]
    ny = nc // 2
    dma = pltpu.SemaphoreType.DMA
    hops = max(ny - 1, 1)
    return pl.pallas_call(
        functools.partial(gather_kernel, nt, nc),
        out_shape=jax.ShapeDtypeStruct((3, HALO + rows, wide), jnp.bfloat16),
        in_specs=[pl.BlockSpec(memory_space=pl.ANY)] * 2 + [pl.BlockSpec(memory_space=pltpu.VMEM)],
        out_specs=pl.BlockSpec(memory_space=pltpu.VMEM),
        scratch_shapes=[
            pltpu.VMEM((nt, rows, feats), jnp.bfloat16),
            pltpu.VMEM((3, nc * deep, wide), jnp.bfloat16),
            pltpu.VMEM((rows // PIECES, nt * feats), jnp.bfloat16),
            dma((2,)),
            dma((2, nt - 1, PIECES)),
            dma((2, nt - 1, PIECES)),
            dma((2, hops, 3)),
            dma((2, hops, 3)),
            dma((2, hops, 3)),
            dma((2, hops, 3)),
            dma((2, hops, 3, 2)),
            dma((2, hops, 3, 2)),
            dma,
            dma,
            dma,
            dma,
        ],
        compiler_params=pltpu.CompilerParams(collective_id=0, has_side_effects=True, vmem_limit_bytes=52 << 20),
        name="gather_project",
    )(tokens, in_weight, gain)


def transforms():
    k = np.arange(POINTS // 2)[:, None]
    n = np.arange(POINTS)[None, :]
    angle = 2 * np.pi * ((k * n) % POINTS) / POINTS
    cos, sin = np.cos(angle), -np.sin(angle)
    sin[0] = np.where(np.arange(POINTS) % 2 == 0, 1.0, -1.0)
    forward = np.concatenate([cos, sin], axis=0)
    weight = np.full((POINTS, 1), 2.0 / POINTS)
    weight[0] = weight[POINTS // 2] = 1.0 / POINTS
    back = (forward * weight).T[BLOCK:]
    return forward.astype(np.float32), back.astype(np.float32)


def conv_kernel(bounds, proj, taps, spec, skip, dist, seg, fwd, back, out, inner, gate):
    blocks = inner.shape[0] // BLOCK
    ntaps = taps.shape[1]

    def featurize(b, carry):
        start = pl.multiple_of(b * BLOCK, BLOCK)
        near = dist[pl.ds(pl.multiple_of(start + 16, 16), BLOCK), :]
        sums = [None] * 3
        valid = [near >= lag for lag in range(ntaps)]
        for g in range(3):
            whole = proj[g, pl.ds(start, BLOCK + 16), :].astype(jnp.float32)
            total = None
            for lag in range(ntaps):
                term = taps[g, lag : lag + 1, :] * whole[16 - lag : 16 - lag + BLOCK]
                term = jnp.where(valid[lag], term, 0.0)
                total = term if total is None else total + term
            sums[g] = total
        inner[pl.ds(start, BLOCK), :] = (sums[1] * sums[2]).astype(jnp.bfloat16)
        gate[pl.ds(start, BLOCK), :] = sums[0]
        return carry

    lax.fori_loop(0, blocks, featurize, 0)
    f = fwd[...]
    w = back[...]
    hb = POINTS // 2

    def filter_block(b, carry):
        start = pl.multiple_of(b * BLOCK, BLOCK)
        window = inner[pl.ds(start, 2 * BLOCK), :].astype(jnp.float32)
        ids = seg[pl.ds(pl.multiple_of(start + 16, 16), 2 * BLOCK), :]
        mine = ids[BLOCK:]

        def one(s, acc):
            x = jnp.where(ids == s, window, 0.0).astype(jnp.bfloat16)
            z = jnp.dot(f, x, preferred_element_type=jnp.float32)
            a, bb = z[:hb], z[hb:]
            re = a * spec[0] - bb * spec[1]
            im = a * spec[1] + bb * spec[2]
            prod = jnp.concatenate([re, im], axis=0).astype(jnp.bfloat16)
            return jnp.where(mine == s, jnp.dot(w, prod, preferred_element_type=jnp.float32), acc)

        conv = lax.fori_loop(bounds[b], bounds[blocks + b] + 1, one, jnp.zeros((BLOCK, out.shape[1]), jnp.float32))
        here = pl.ds(pl.multiple_of(start + BLOCK, BLOCK), BLOCK)
        mixed = gate[here, :] * (conv + skip[...] * window[BLOCK:])
        out[pl.ds(start, BLOCK), :] = mixed.astype(jnp.bfloat16)
        return carry

    lax.fori_loop(0, blocks - 1, filter_block, 0)


def filter_gate(proj, taps, spec, skip, dist, seg, bounds, fwd, back):
    _, ext, wide = proj.shape
    rows = ext - HALO
    cols = 256
    whole = lambda shape: pl.BlockSpec(shape, lambda j, b: (0,) * len(shape))
    return pl.pallas_call(
        conv_kernel,
        grid_spec=pltpu.PrefetchScalarGridSpec(
            num_scalar_prefetch=1,
            grid=(wide // cols,),
            in_specs=[
                pl.BlockSpec((3, ext, cols), lambda j, b: (0, 0, j)),
                pl.BlockSpec((3, taps.shape[1], cols), lambda j, b: (0, 0, j)),
                pl.BlockSpec((3, POINTS // 2, cols), lambda j, b: (0, 0, j)),
                pl.BlockSpec((1, cols), lambda j, b: (0, j)),
                whole((ext, cols)),
                whole((ext, cols)),
                whole((POINTS, POINTS)),
                whole((BLOCK, POINTS)),
            ],
            out_specs=pl.BlockSpec((rows, cols), lambda j, b: (0, j)),
            scratch_shapes=[
                pltpu.VMEM((rows + BLOCK, cols), jnp.bfloat16),
                pltpu.VMEM((rows + BLOCK, cols), jnp.float32),
            ],
        ),
        out_shape=jax.ShapeDtypeStruct((rows, wide), jnp.bfloat16),
        compiler_params=pltpu.CompilerParams(vmem_limit_bytes=40 << 20),
        name="filter_gate",
    )(bounds, proj, taps, spec, skip, dist, seg, fwd, back)


def distances(segment_ids):
    count = segment_ids.shape[0]
    places = jnp.arange(count, dtype=jnp.int32)
    earlier = jnp.concatenate([segment_ids[:1] - 1, segment_ids[:-1]])
    starts = jnp.where(segment_ids != earlier, places, jnp.zeros_like(places))
    return places - lax.cummax(starts, axis=0)


def per_device(nt, nc, tokens, norm_gain, in_weight, short_taps, long_filter, skip_bias, segment_ids):
    rows = tokens.shape[0]
    first = lax.axis_index("context") * rows
    pad = jnp.full((HALO,), -1, jnp.int32)
    ids = lax.dynamic_slice_in_dim(jnp.concatenate([pad, segment_ids]), first, rows + HALO, 0)
    dist = lax.dynamic_slice_in_dim(jnp.concatenate([pad, distances(segment_ids)]), first, rows + HALO, 0)
    bounds = jnp.concatenate([ids[HALO::BLOCK], ids[HALO + BLOCK - 1 :: BLOCK]])
    spread = lambda v: jnp.broadcast_to(v[:, None], (rows + HALO, 256))
    forward, back = transforms()
    full = jnp.dot(forward[:, : long_filter.shape[1]], long_filter.T, precision=lax.Precision.HIGHEST)
    top = (jnp.arange(BLOCK) == 0)[:, None]
    re, im = full[:BLOCK], full[BLOCK:]
    spec = jnp.stack([re, jnp.where(top, 0.0, im), jnp.where(top, im, re)])
    last = jnp.zeros((1,), jnp.int32)
    n = rows // BLOCK
    bounds = jnp.concatenate([bounds[:n], last, bounds[n:]])
    proj = project_all(nt, nc, tokens, in_weight, norm_gain[None, :])
    return filter_gate(
        proj, short_taps, spec, skip_bias[None, :], spread(dist), spread(ids), bounds,
        jnp.asarray(forward, jnp.bfloat16), jnp.asarray(back, jnp.bfloat16),
    )


def solution(mesh):
    placed = (
        P(("dp", "context"), "tensor"),
        P(),
        P(None, "context", "tensor"),
        P(None, None, "tensor"),
        P("tensor", None),
        P("tensor"),
        P("dp"),
    )
    return jax.shard_map(
        functools.partial(per_device, mesh.shape["tensor"], mesh.shape["context"]),
        mesh=mesh,
        in_specs=placed,
        out_specs=P(("dp", "context"), "tensor"),
        check_vma=False,
    )
```

```python
import functools
import math

import jax
import jax.numpy as jnp
import numpy as np
from jax import lax
from jax.experimental import pallas as pl
from jax.experimental.pallas import tpu as pltpu
from jax.sharding import PartitionSpec as P

MESH = pl.DeviceIdType.MESH
PIECES = 8
HALO = 144
BLOCK = 128
POINTS = 256


def gather_kernel(nt, nc, x_in, w_in, gain, taps, dist, inner, gate, xbuf, wbuf, normed, out, strip, loc, xs, xr, ys, yr, ps, pr, cs, cr, os_, or_, hs, hr):
    d = lax.axis_index("dp")
    i = lax.axis_index("context")
    t = lax.axis_index("tensor")
    y, c = i // 2, i % 2
    ny = nc // 2
    rows = x_in.shape[0] // PIECES
    deep = w_in.shape[1]
    half = deep // 2
    sib = (d, i + 1 - 2 * c, t)
    peer = (1 - d, i, t)

    mine_x = pltpu.make_async_copy(x_in, xbuf.at[t], loc.at[0])
    mine_w = pltpu.make_async_copy(w_in, wbuf.at[:, pl.ds(i * deep, deep), :], loc.at[1])
    mine_x.start()
    mine_w.start()

    bar = pltpu.get_barrier_semaphore()

    def greet(dev):
        pl.semaphore_signal(bar, inc=1, device_id=dev, device_id_type=MESH)

    greet(sib)
    greet(peer)
    peers = jnp.int32(2)
    for cond, dev in (
        (t > 0, (d, i, t - 1)),
        (t < nt - 1, (d, i, t + 1)),
        (y > 0, (d, i - 2, t)),
        (y < ny - 1, (d, i + 2, t)),
        ((c == 0) & (i > 0), (d, i - 1, t)),
        ((c == 1) & (i < nc - 1), (d, i + 1, t)),
    ):
        peers = peers + cond.astype(jnp.int32)

        @pl.when(cond)
        def _():
            greet(dev)

    pl.semaphore_wait(bar, peers)

    def spot(r):
        return pl.multiple_of(lax.rem(r + PIECES - 2, PIECES) * rows, rows)

    def xcopy(side, hop, r, block, first):
        place = pl.ds(spot(r), rows)
        dst = xbuf.at[block, place, :]
        src = x_in.at[place, :] if first else dst
        to = (d, i, t + 1) if side == 0 else (d, i, t - 1)
        return pltpu.make_async_remote_copy(src, dst, xs.at[side, hop, r], xr.at[side, hop, r], device_id=to, device_id_type=MESH)

    def x_sends(side, hop):
        return (t < nt - 1) & (t - hop >= 0) if side == 0 else (t > 0) & (t + hop < nt)

    def x_takes(side, hop):
        return t - 1 - hop >= 0 if side == 0 else t + 1 + hop < nt

    def x_sent(side, hop):
        return t - hop if side == 0 else t + hop

    def x_taken(side, hop):
        return t - 1 - hop if side == 0 else t + 1 + hop

    def when(cond, f):
        pl.when(cond)(f)

    def wspan(block, part):
        return pl.ds(pl.multiple_of(block * deep + part * half, half), half)

    def ycopy(side, hop, g, yb, first):
        place = wspan(yb * 2 + c, d)
        dst = wbuf.at[g, place, :]
        src = w_in.at[g, pl.ds(pl.multiple_of(d * half, half), half), :] if first else dst
        to = (d, i + 2, t) if side == 0 else (d, i - 2, t)
        return pltpu.make_async_remote_copy(src, dst, ys.at[side, hop, g], yr.at[side, hop, g], device_id=to, device_id_type=MESH)

    def y_sends(side, hop):
        return (y < ny - 1) & (y - hop >= 0) if side == 0 else (y > 0) & (y + hop < ny)

    def y_takes(side, hop):
        return y - 1 - hop >= 0 if side == 0 else y + 1 + hop < ny

    def y_sent(side, hop):
        return y - hop if side == 0 else y + hop

    def y_taken(side, hop):
        return y - 1 - hop if side == 0 else y + 1 + hop

    def pcopy(side, hop, g, yb, part):
        at = wbuf.at[g, wspan(yb * 2 + c, part), :]
        return pltpu.make_async_remote_copy(at, at, ps.at[side, hop, g], pr.at[side, hop, g], device_id=peer, device_id_type=MESH)

    def ccopy(side, hop, g, via, yb, core, part):
        at = wbuf.at[g, wspan(yb * 2 + core, part), :]
        return pltpu.make_async_remote_copy(at, at, cs.at[side, hop, g, via], cr.at[side, hop, g, via], device_id=sib, device_id_type=MESH)

    def ocopy(block):
        at = wbuf.at[:, pl.ds(pl.multiple_of(block * deep, deep), deep), :]
        return pltpu.make_async_remote_copy(w_in, at, os_, or_, device_id=sib, device_id_type=MESH)

    sides = (0, 1)

    for g in range(3):
        for side in sides:
            when(y_sends(side, 0), lambda: ycopy(side, 0, g, y, True).start())

    def start_own(r, carry):
        for side in sides:
            when(x_sends(side, 0), lambda: xcopy(side, 0, r, t, True).start())
        return carry

    lax.fori_loop(0, PIECES, start_own, 0)
    ocopy(i).start()

    def pass_x(step, carry):
        hop, r = step // PIECES, step % PIECES
        for side in sides:
            @pl.when(x_takes(side, hop))
            def _():
                xcopy(side, hop, r, x_taken(side, hop), False).wait_recv()

            when(x_sends(side, hop + 1), lambda: xcopy(side, hop + 1, r, x_sent(side, hop + 1), False).start())
        return carry

    def pass_w(g):
        for hop in range(ny - 1):
            for side in sides:
                @pl.when(y_takes(side, hop))
                def _():
                    yb = y_taken(side, hop)
                    ycopy(side, hop, g, yb, False).wait_recv()
                    pcopy(side, hop, g, yb, d).start()
                    ccopy(side, hop, g, 0, yb, c, d).start()

                if hop + 1 < ny - 1:
                    when(y_sends(side, hop + 1), lambda: ycopy(side, hop + 1, g, y_sent(side, hop + 1), False).start())

    def pass_p(g):
        for hop in range(ny - 1):
            for side in sides:
                @pl.when(y_takes(side, hop))
                def _():
                    yb = y_taken(side, hop)
                    pcopy(side, hop, g, yb, 1 - d).wait_recv()
                    ccopy(side, hop, g, 1, yb, c, 1 - d).start()

    steps = (nt - 2) * PIECES
    cuts = (steps // 4, steps // 2, 3 * steps // 4)
    at = 0
    for g in range(3):
        lax.fori_loop(at, cuts[g], pass_x, 0)
        at = cuts[g]
        pass_w(g)
        if g:
            pass_p(g - 1)
    lax.fori_loop(at, steps, pass_x, 0)
    pass_p(2)

    mine_x.wait()
    mine_w.wait()
    ocopy(sib[1]).wait_recv()
    for g in range(3):
        for hop in range(ny - 1):
            for side in sides:
                @pl.when(y_takes(side, hop))
                def _():
                    yb = y_taken(side, hop)
                    ccopy(side, hop, g, 0, yb, 1 - c, d).wait_recv()
                    ccopy(side, hop, g, 1, yb, 1 - c, 1 - d).wait_recv()

    wide = w_in.shape[2]
    tile = min(512, wide)
    feats = x_in.shape[1]

    def project(r):
        for side in sides:
            when(x_takes(side, nt - 2), lambda: xcopy(side, nt - 2, r, x_taken(side, nt - 2), False).wait_recv())
        place = pl.ds(spot(r), rows)
        total = jnp.zeros((rows, 1), jnp.float32)
        for k in range(nt):
            v = xbuf[k, place, :].astype(jnp.float32)
            total = total + jnp.sum(v * v, axis=1, keepdims=True)
        scale = lax.rsqrt(total * (1.0 / (feats * nt)) + 1e-06)
        for k in range(nt):
            v = xbuf[k, place, :].astype(jnp.float32)
            cols = pl.ds(k * feats, feats)
            normed[:, cols] = (v * scale * gain[:, cols]).astype(jnp.bfloat16)
        to = pl.ds(pl.multiple_of(HALO + spot(r), 16), rows)

        def one(n, carry):
            g = n // (wide // tile)
            cols = pl.ds(pl.multiple_of((n % (wide // tile)) * tile, tile), tile)
            out[g, to, cols] = jnp.dot(normed[...], wbuf[g, :, cols], preferred_element_type=jnp.float32).astype(jnp.bfloat16)
            return carry

        lax.fori_loop(0, 3 * (wide // tile), one, 0)

    ntaps = taps.shape[1]

    def featurize(start):
        start = pl.multiple_of(start, BLOCK)
        at = pl.ds(start, BLOCK)

        def column(n, carry):
            cols = pl.ds(pl.multiple_of(n * 128, 128), 128)
            near = dist[pl.ds(pl.multiple_of(start + 16, 16), BLOCK), :]
            sums = [None] * 3
            for g in range(3):
                strip[g] = out[g, pl.ds(start, BLOCK + 16), cols].astype(jnp.float32)
            for lag in range(ntaps):
                valid = near >= lag
                for g in range(3):
                    term = taps[g, lag : lag + 1, cols] * strip[g, 16 - lag : 16 - lag + BLOCK, :]
                    term = jnp.where(valid, term, 0.0)
                    sums[g] = term if lag == 0 else sums[g] + term
            inner[at, cols] = (sums[1] * sums[2]).astype(jnp.bfloat16)
            gate[at, cols] = sums[0]
            return carry

        lax.fori_loop(0, wide // 128, column, 0)

    def project_step(r, carry):
        project(r)
        return carry

    def both(r, carry):
        project(r)
        featurize(BLOCK + spot(r))
        return carry

    total_rows = rows * PIECES

    def hcopy():
        return pltpu.make_async_remote_copy(
            out.at[:, pl.ds(total_rows, HALO), :], out.at[:, pl.ds(0, HALO), :], hs, hr, device_id=(d, i + 1, t), device_id_type=MESH
        )

    @pl.when(i == 0)
    def _():
        out[:, 0:HALO, :] = jnp.zeros((3, HALO, wide), jnp.bfloat16)

    lax.fori_loop(0, 2, project_step, 0)
    when(i < nc - 1, lambda: hcopy().start())
    featurize(BLOCK + (PIECES - 1) * rows)
    lax.fori_loop(2, 4, project_step, 0)
    when(i > 0, lambda: hcopy().wait_recv())
    featurize(0)
    featurize(BLOCK)
    featurize(BLOCK + rows)
    lax.fori_loop(4, PIECES, both, 0)
    featurize(BLOCK + (PIECES - 2) * rows)

    def drain(r, carry):
        for hop in range(nt - 1):
            for side in sides:
                when(x_sends(side, hop), lambda: xcopy(side, hop, r, x_sent(side, hop), False).wait_send())
        return carry

    lax.fori_loop(0, PIECES, drain, 0)
    for g in range(3):
        for hop in range(ny - 1):
            for side in sides:
                when(y_sends(side, hop), lambda: ycopy(side, hop, g, y_sent(side, hop), False).wait_send())

                @pl.when(y_takes(side, hop))
                def _():
                    yb = y_taken(side, hop)
                    pcopy(side, hop, g, yb, d).wait_send()
                    ccopy(side, hop, g, 0, yb, c, d).wait_send()
                    ccopy(side, hop, g, 1, yb, c, 1 - d).wait_send()
    ocopy(i).wait_send()
    when(i < nc - 1, lambda: hcopy().wait_send())


def project_all(nt, nc, tokens, in_weight, gain, taps, dist):
    rows, feats = tokens.shape
    deep, wide = in_weight.shape[1:]
    ny = nc // 2
    dma = pltpu.SemaphoreType.DMA
    hops = max(ny - 1, 1)
    return pl.pallas_call(
        functools.partial(gather_kernel, nt, nc),
        out_shape=(
            jax.ShapeDtypeStruct((BLOCK + rows, wide), jnp.bfloat16),
            jax.ShapeDtypeStruct((BLOCK + rows, wide), jnp.float32),
        ),
        in_specs=[pl.BlockSpec(memory_space=pl.ANY)] * 2 + [pl.BlockSpec(memory_space=pltpu.VMEM)] * 3,
        out_specs=(pl.BlockSpec(memory_space=pltpu.VMEM),) * 2,
        scratch_shapes=[
            pltpu.VMEM((nt, rows, feats), jnp.bfloat16),
            pltpu.VMEM((3, nc * deep, wide), jnp.bfloat16),
            pltpu.VMEM((rows // PIECES, nt * feats), jnp.bfloat16),
            pltpu.VMEM((3, HALO + rows, wide), jnp.bfloat16),
            pltpu.VMEM((3, BLOCK + 16, 128), jnp.float32),
            dma((2,)),
            dma((2, nt - 1, PIECES)),
            dma((2, nt - 1, PIECES)),
            dma((2, hops, 3)),
            dma((2, hops, 3)),
            dma((2, hops, 3)),
            dma((2, hops, 3)),
            dma((2, hops, 3, 2)),
            dma((2, hops, 3, 2)),
            dma,
            dma,
            dma,
            dma,
        ],
        compiler_params=pltpu.CompilerParams(collective_id=0, has_side_effects=True, vmem_limit_bytes=56 << 20),
        name="gather_project",
    )(tokens, in_weight, gain, taps, dist)


def transforms():
    k = np.arange(POINTS // 2)[:, None]
    n = np.arange(POINTS)[None, :]
    angle = 2 * np.pi * ((k * n) % POINTS) / POINTS
    cos, sin = np.cos(angle), -np.sin(angle)
    sin[0] = np.where(np.arange(POINTS) % 2 == 0, 1.0, -1.0)
    forward = np.concatenate([cos, sin], axis=0)
    weight = np.full((POINTS, 1), 2.0 / POINTS)
    weight[0] = weight[POINTS // 2] = 1.0 / POINTS
    back = (forward * weight).T[BLOCK:]
    return forward.astype(np.float32), back.astype(np.float32)


def conv_kernel(bounds, inner, gate, filt, skip, seg, wave, fwd, back, out, spec):
    blocks = inner.shape[0] // BLOCK
    wide = out.shape[1]
    full = lax.dot_general(
        wave[...], filt[...], (((1,), (1,)), ((), ())), precision=lax.Precision.HIGHEST, preferred_element_type=jnp.float32
    )
    re0, im0 = full[:BLOCK], full[BLOCK:]
    top = lax.broadcasted_iota(jnp.int32, re0.shape, 0) == 0
    spec[0] = re0
    spec[1] = jnp.where(top, 0.0, im0)
    spec[2] = jnp.where(top, im0, re0)
    f = fwd[...]
    w = back[...]
    hb = POINTS // 2

    def filter_block(b, carry):
        start = pl.multiple_of(b * BLOCK, BLOCK)
        window = inner[pl.ds(start, 2 * BLOCK), :].astype(jnp.float32)
        ids = seg[pl.ds(pl.multiple_of(start + 16, 16), 2 * BLOCK), :]
        ids = jnp.concatenate([ids] * (wide // 128), axis=1)
        mine = ids[BLOCK:]

        def one(s, acc):
            x = jnp.where(ids == s, window, 0.0).astype(jnp.bfloat16)
            z = jnp.dot(f, x, preferred_element_type=jnp.float32)
            a, bb = z[:hb], z[hb:]
            re = a * spec[0] - bb * spec[1]
            im = a * spec[1] + bb * spec[2]
            prod = jnp.concatenate([re, im], axis=0).astype(jnp.bfloat16)
            return jnp.where(mine == s, jnp.dot(w, prod, preferred_element_type=jnp.float32), acc)

        conv = lax.fori_loop(bounds[b], bounds[blocks + b] + 1, one, jnp.zeros((BLOCK, out.shape[1]), jnp.float32))
        here = pl.ds(pl.multiple_of(start + BLOCK, BLOCK), BLOCK)
        mixed = gate[here, :] * (conv + skip[...] * window[BLOCK:])
        out[pl.ds(start, BLOCK), :] = mixed.astype(jnp.bfloat16)
        return carry

    lax.fori_loop(0, blocks - 1, filter_block, 0)


def filter_gate(inner, gate, filt, skip, seg, bounds, wave, fwd, back):
    ext, wide = inner.shape
    rows = ext - BLOCK
    cols = min(512, wide)
    column = lambda n: pl.BlockSpec((n, cols), lambda j, b: (0, j))
    whole = lambda v: pl.BlockSpec(v.shape, lambda j, b: (0,) * v.ndim)
    return pl.pallas_call(
        conv_kernel,
        grid_spec=pltpu.PrefetchScalarGridSpec(
            num_scalar_prefetch=1,
            grid=(wide // cols,),
            in_specs=[
                column(ext),
                column(ext),
                pl.BlockSpec((cols, filt.shape[1]), lambda j, b: (j, 0)),
                column(1),
                whole(seg),
                whole(wave),
                whole(fwd),
                whole(back),
            ],
            out_specs=column(rows),
            scratch_shapes=[pltpu.VMEM((3, BLOCK, cols), jnp.float32)],
        ),
        out_shape=jax.ShapeDtypeStruct((rows, wide), jnp.bfloat16),
        compiler_params=pltpu.CompilerParams(vmem_limit_bytes=40 << 20),
        name="filter_gate",
    )(bounds, inner, gate, filt, skip, seg, wave, fwd, back)


def distances(segment_ids):
    count = segment_ids.shape[0]
    places = jnp.arange(count, dtype=jnp.int32)
    earlier = jnp.concatenate([segment_ids[:1] - 1, segment_ids[:-1]])
    starts = jnp.where(segment_ids != earlier, places, jnp.zeros_like(places))
    return places - lax.cummax(starts, axis=0)


def per_device(nt, nc, tokens, norm_gain, in_weight, short_taps, long_filter, skip_bias, segment_ids):
    rows = tokens.shape[0]
    first = lax.axis_index("context") * rows
    pad = jnp.full((HALO,), -1, jnp.int32)
    ids = lax.dynamic_slice_in_dim(jnp.concatenate([pad, segment_ids]), first, rows + HALO, 0)
    dist = lax.dynamic_slice_in_dim(jnp.concatenate([pad, distances(segment_ids)]), first, rows + HALO, 0)
    bounds = jnp.concatenate([ids[HALO::BLOCK], ids[HALO + BLOCK - 1 :: BLOCK]])
    spread = lambda v: jnp.broadcast_to(v[:, None], (rows + HALO, 128))
    forward, back = transforms()
    last = jnp.zeros((1,), jnp.int32)
    n = rows // BLOCK
    bounds = jnp.concatenate([bounds[:n], last, bounds[n:]])
    inner, gate = project_all(nt, nc, tokens, in_weight, norm_gain[None, :], short_taps, spread(dist))
    return filter_gate(
        inner, gate, long_filter, skip_bias[None, :], spread(ids), bounds,
        jnp.asarray(forward[:, : long_filter.shape[1]]), jnp.asarray(forward, jnp.bfloat16), jnp.asarray(back, jnp.bfloat16),
    )


def solution(mesh):
    placed = (
        P(("dp", "context"), "tensor"),
        P(),
        P(None, "context", "tensor"),
        P(None, None, "tensor"),
        P("tensor", None),
        P("tensor"),
        P("dp"),
    )
    return jax.shard_map(
        functools.partial(per_device, mesh.shape["tensor"], mesh.shape["context"]),
        mesh=mesh,
        in_specs=placed,
        out_specs=P(("dp", "context"), "tensor"),
        check_vma=False,
    )
```

```python
import functools
import math

import jax
import jax.numpy as jnp
import numpy as np
from jax import lax
from jax.experimental import pallas as pl
from jax.experimental.pallas import tpu as pltpu
from jax.sharding import PartitionSpec as P

MESH = pl.DeviceIdType.MESH
PIECES = 8
HALO = 144
BLOCK = 128
POINTS = 256


def gather_kernel(nt, nc, x_in, w_in, gain, taps, dist, inner_out, gate_out, xbuf, wbuf, normed, out, strip, inner, gate, flush, loc, xs, xr, ys, yr, ps, pr, cs, cr, os_, or_, hs, hr):
    d = lax.axis_index("dp")
    i = lax.axis_index("context")
    t = lax.axis_index("tensor")
    y, c = i // 2, i % 2
    ny = nc // 2
    rows = x_in.shape[0] // PIECES
    deep = w_in.shape[1]
    half = deep // 2
    sib = (d, i + 1 - 2 * c, t)
    peer = (1 - d, i, t)

    mine_x = pltpu.make_async_copy(x_in, xbuf.at[t], loc.at[0])
    mine_w = pltpu.make_async_copy(w_in, wbuf.at[:, pl.ds(i * deep, deep), :], loc.at[1])
    mine_x.start()
    mine_w.start()

    bar = pltpu.get_barrier_semaphore()

    def greet(dev):
        pl.semaphore_signal(bar, inc=1, device_id=dev, device_id_type=MESH)

    greet(sib)
    greet(peer)
    peers = jnp.int32(2)
    for cond, dev in (
        (t > 0, (d, i, t - 1)),
        (t < nt - 1, (d, i, t + 1)),
        (y > 0, (d, i - 2, t)),
        (y < ny - 1, (d, i + 2, t)),
        ((c == 0) & (i > 0), (d, i - 1, t)),
        ((c == 1) & (i < nc - 1), (d, i + 1, t)),
    ):
        peers = peers + cond.astype(jnp.int32)

        @pl.when(cond)
        def _():
            greet(dev)

    pl.semaphore_wait(bar, peers)

    def spot(r):
        return pl.multiple_of(lax.rem(r + PIECES - 2, PIECES) * rows, rows)

    def xcopy(side, hop, r, block, first):
        place = pl.ds(spot(r), rows)
        dst = xbuf.at[block, place, :]
        src = x_in.at[place, :] if first else dst
        to = (d, i, t + 1) if side == 0 else (d, i, t - 1)
        return pltpu.make_async_remote_copy(src, dst, xs.at[side, hop, r], xr.at[side, hop, r], device_id=to, device_id_type=MESH)

    def x_sends(side, hop):
        return (t < nt - 1) & (t - hop >= 0) if side == 0 else (t > 0) & (t + hop < nt)

    def x_takes(side, hop):
        return t - 1 - hop >= 0 if side == 0 else t + 1 + hop < nt

    def x_sent(side, hop):
        return t - hop if side == 0 else t + hop

    def x_taken(side, hop):
        return t - 1 - hop if side == 0 else t + 1 + hop

    def when(cond, f):
        pl.when(cond)(f)

    def wspan(block, part):
        return pl.ds(pl.multiple_of(block * deep + part * half, half), half)

    def ycopy(side, hop, g, yb, first):
        place = wspan(yb * 2 + c, d)
        dst = wbuf.at[g, place, :]
        src = w_in.at[g, pl.ds(pl.multiple_of(d * half, half), half), :] if first else dst
        to = (d, i + 2, t) if side == 0 else (d, i - 2, t)
        return pltpu.make_async_remote_copy(src, dst, ys.at[side, hop, g], yr.at[side, hop, g], device_id=to, device_id_type=MESH)

    def y_sends(side, hop):
        return (y < ny - 1) & (y - hop >= 0) if side == 0 else (y > 0) & (y + hop < ny)

    def y_takes(side, hop):
        return y - 1 - hop >= 0 if side == 0 else y + 1 + hop < ny

    def y_sent(side, hop):
        return y - hop if side == 0 else y + hop

    def y_taken(side, hop):
        return y - 1 - hop if side == 0 else y + 1 + hop

    def pcopy(side, hop, g, yb, part):
        at = wbuf.at[g, wspan(yb * 2 + c, part), :]
        return pltpu.make_async_remote_copy(at, at, ps.at[side, hop, g], pr.at[side, hop, g], device_id=peer, device_id_type=MESH)

    def ccopy(side, hop, g, via, yb, core, part):
        at = wbuf.at[g, wspan(yb * 2 + core, part), :]
        return pltpu.make_async_remote_copy(at, at, cs.at[side, hop, g, via], cr.at[side, hop, g, via], device_id=sib, device_id_type=MESH)

    def ocopy(block):
        at = wbuf.at[:, pl.ds(pl.multiple_of(block * deep, deep), deep), :]
        return pltpu.make_async_remote_copy(w_in, at, os_, or_, device_id=sib, device_id_type=MESH)

    sides = (0, 1)

    for g in range(3):
        for side in sides:
            when(y_sends(side, 0), lambda: ycopy(side, 0, g, y, True).start())

    def start_own(r, carry):
        for side in sides:
            when(x_sends(side, 0), lambda: xcopy(side, 0, r, t, True).start())
        return carry

    lax.fori_loop(0, PIECES, start_own, 0)
    ocopy(i).start()

    def pass_x(step, carry):
        hop, r = step // PIECES, step % PIECES
        for side in sides:
            @pl.when(x_takes(side, hop))
            def _():
                xcopy(side, hop, r, x_taken(side, hop), False).wait_recv()

            when(x_sends(side, hop + 1), lambda: xcopy(side, hop + 1, r, x_sent(side, hop + 1), False).start())
        return carry

    def pass_w(g):
        for hop in range(ny - 1):
            for side in sides:
                @pl.when(y_takes(side, hop))
                def _():
                    yb = y_taken(side, hop)
                    ycopy(side, hop, g, yb, False).wait_recv()
                    pcopy(side, hop, g, yb, d).start()
                    ccopy(side, hop, g, 0, yb, c, d).start()

                if hop + 1 < ny - 1:
                    when(y_sends(side, hop + 1), lambda: ycopy(side, hop + 1, g, y_sent(side, hop + 1), False).start())

    def pass_p(g):
        for hop in range(ny - 1):
            for side in sides:
                @pl.when(y_takes(side, hop))
                def _():
                    yb = y_taken(side, hop)
                    pcopy(side, hop, g, yb, 1 - d).wait_recv()
                    ccopy(side, hop, g, 1, yb, c, 1 - d).start()

    steps = (nt - 2) * PIECES
    cuts = (steps - 8, steps - 6, steps - 5)
    at = 0
    for g in range(3):
        lax.fori_loop(at, cuts[g], pass_x, 0)
        at = cuts[g]
        pass_w(g)
        if g:
            pass_p(g - 1)
    lax.fori_loop(at, steps - 4, pass_x, 0)
    pass_p(2)

    mine_x.wait()
    mine_w.wait()
    ocopy(sib[1]).wait_recv()
    for g in range(3):
        for hop in range(ny - 1):
            for side in sides:
                @pl.when(y_takes(side, hop))
                def _():
                    yb = y_taken(side, hop)
                    ccopy(side, hop, g, 0, yb, 1 - c, d).wait_recv()
                    ccopy(side, hop, g, 1, yb, 1 - c, 1 - d).wait_recv()

    wide = w_in.shape[2]
    tile = min(512, wide)
    feats = x_in.shape[1]

    def project(r):
        for side in sides:
            when(x_takes(side, nt - 2), lambda: xcopy(side, nt - 2, r, x_taken(side, nt - 2), False).wait_recv())
        place = pl.ds(spot(r), rows)
        total = jnp.zeros((rows, 1), jnp.float32)
        for k in range(nt):
            v = xbuf[k, place, :].astype(jnp.float32)
            total = total + jnp.sum(v * v, axis=1, keepdims=True)
        scale = lax.rsqrt(total * (1.0 / (feats * nt)) + 1e-06)
        for k in range(nt):
            v = xbuf[k, place, :].astype(jnp.float32)
            cols = pl.ds(k * feats, feats)
            normed[:, cols] = (v * scale * gain[:, cols]).astype(jnp.bfloat16)
        to = pl.ds(pl.multiple_of(HALO + spot(r), 16), rows)

        def one(n, carry):
            g = n // (wide // tile)
            cols = pl.ds(pl.multiple_of((n % (wide // tile)) * tile, tile), tile)
            out[g, to, cols] = jnp.dot(normed[...], wbuf[g, :, cols], preferred_element_type=jnp.float32).astype(jnp.bfloat16)
            return carry

        lax.fori_loop(0, 3 * (wide // tile), one, 0)

    ntaps = taps.shape[1]

    def flushes(start):
        at, k = pl.ds(start, BLOCK), start // BLOCK
        return (
            pltpu.make_async_copy(inner.at[at, :], inner_out.at[at, :], flush.at[0, k]),
            pltpu.make_async_copy(gate.at[at, :], gate_out.at[at, :], flush.at[1, k]),
        )

    def featurize(start):
        start = pl.multiple_of(start, BLOCK)
        at = pl.ds(start, BLOCK)

        def column(n, carry):
            cols = pl.ds(pl.multiple_of(n * 128, 128), 128)
            near = dist[pl.ds(pl.multiple_of(start + 16, 16), BLOCK), :]
            sums = [None] * 3
            for g in range(3):
                strip[g] = out[g, pl.ds(start, BLOCK + 16), cols].astype(jnp.float32)
            for lag in range(ntaps):
                valid = near >= lag
                for g in range(3):
                    term = taps[g, lag : lag + 1, cols] * strip[g, 16 - lag : 16 - lag + BLOCK, :]
                    term = jnp.where(valid, term, 0.0)
                    sums[g] = term if lag == 0 else sums[g] + term
            inner[at, cols] = (sums[1] * sums[2]).astype(jnp.bfloat16)
            gate[at, cols] = sums[0]
            return carry

        lax.fori_loop(0, wide // 128, column, 0)
        for copy in flushes(start):
            copy.start()

    def project_step(r, carry):
        project(r)
        return carry

    def pass_project(q, carry):
        pass_x(steps - 4 + q, 0)
        project(q)
        return carry

    def both(r, carry):
        project(r)
        featurize(BLOCK + spot(r))
        return carry

    total_rows = rows * PIECES

    def hcopy():
        return pltpu.make_async_remote_copy(
            out.at[:, pl.ds(total_rows, HALO), :], out.at[:, pl.ds(0, HALO), :], hs, hr, device_id=(d, i + 1, t), device_id_type=MESH
        )

    @pl.when(i == 0)
    def _():
        out[:, 0:HALO, :] = jnp.zeros((3, HALO, wide), jnp.bfloat16)

    lax.fori_loop(0, 2, pass_project, 0)
    when(i < nc - 1, lambda: hcopy().start())
    lax.fori_loop(2, 4, pass_project, 0)
    featurize(BLOCK + (PIECES - 1) * rows)
    when(i > 0, lambda: hcopy().wait_recv())
    featurize(0)
    featurize(BLOCK)
    featurize(BLOCK + rows)
    lax.fori_loop(4, PIECES, both, 0)
    featurize(BLOCK + (PIECES - 2) * rows)

    def drain(r, carry):
        for hop in range(nt - 1):
            for side in sides:
                when(x_sends(side, hop), lambda: xcopy(side, hop, r, x_sent(side, hop), False).wait_send())
        return carry

    lax.fori_loop(0, PIECES, drain, 0)
    for g in range(3):
        for hop in range(ny - 1):
            for side in sides:
                when(y_sends(side, hop), lambda: ycopy(side, hop, g, y_sent(side, hop), False).wait_send())

                @pl.when(y_takes(side, hop))
                def _():
                    yb = y_taken(side, hop)
                    pcopy(side, hop, g, yb, d).wait_send()
                    ccopy(side, hop, g, 0, yb, c, d).wait_send()
                    ccopy(side, hop, g, 1, yb, c, 1 - d).wait_send()
    ocopy(i).wait_send()
    when(i < nc - 1, lambda: hcopy().wait_send())

    def flushed(k, carry):
        for copy in flushes(pl.multiple_of(k * BLOCK, BLOCK)):
            copy.wait()
        return carry

    lax.fori_loop(0, 1 + total_rows // BLOCK, flushed, 0)


def project_all(nt, nc, tokens, in_weight, gain, taps, dist):
    rows, feats = tokens.shape
    deep, wide = in_weight.shape[1:]
    ny = nc // 2
    dma = pltpu.SemaphoreType.DMA
    hops = max(ny - 1, 1)
    return pl.pallas_call(
        functools.partial(gather_kernel, nt, nc),
        out_shape=(
            jax.ShapeDtypeStruct((BLOCK + rows, wide), jnp.bfloat16),
            jax.ShapeDtypeStruct((BLOCK + rows, wide), jnp.float32),
        ),
        in_specs=[pl.BlockSpec(memory_space=pl.ANY)] * 2 + [pl.BlockSpec(memory_space=pltpu.VMEM)] * 3,
        out_specs=(pl.BlockSpec(memory_space=pl.ANY),) * 2,
        scratch_shapes=[
            pltpu.VMEM((nt, rows, feats), jnp.bfloat16),
            pltpu.VMEM((3, nc * deep, wide), jnp.bfloat16),
            pltpu.VMEM((rows // PIECES, nt * feats), jnp.bfloat16),
            pltpu.VMEM((3, HALO + rows, wide), jnp.bfloat16),
            pltpu.VMEM((3, BLOCK + 16, 128), jnp.float32),
            pltpu.VMEM((BLOCK + rows, wide), jnp.bfloat16),
            pltpu.VMEM((BLOCK + rows, wide), jnp.float32),
            dma((2, 1 + rows // BLOCK)),
            dma((2,)),
            dma((2, nt - 1, PIECES)),
            dma((2, nt - 1, PIECES)),
            dma((2, hops, 3)),
            dma((2, hops, 3)),
            dma((2, hops, 3)),
            dma((2, hops, 3)),
            dma((2, hops, 3, 2)),
            dma((2, hops, 3, 2)),
            dma,
            dma,
            dma,
            dma,
        ],
        compiler_params=pltpu.CompilerParams(collective_id=0, has_side_effects=True, vmem_limit_bytes=56 << 20),
        name="gather_project",
    )(tokens, in_weight, gain, taps, dist)


def transforms():
    k = np.arange(POINTS // 2)[:, None]
    n = np.arange(POINTS)[None, :]
    angle = 2 * np.pi * ((k * n) % POINTS) / POINTS
    cos, sin = np.cos(angle), -np.sin(angle)
    sin[0] = np.where(np.arange(POINTS) % 2 == 0, 1.0, -1.0)
    forward = np.concatenate([cos, sin], axis=0)
    weight = np.full((POINTS, 1), 2.0 / POINTS)
    weight[0] = weight[POINTS // 2] = 1.0 / POINTS
    back = (forward * weight).T[BLOCK:]
    return forward.astype(np.float32), back.astype(np.float32)


def conv_kernel(bounds, inner, gate, filt, skip, seg, lines, wave, fwd, back, out, spec):
    blocks = inner.shape[0] // BLOCK
    wide = out.shape[1]
    full = lax.dot_general(
        wave[...], filt[...], (((1,), (1,)), ((), ())), precision=lax.Precision.HIGHEST, preferred_element_type=jnp.float32
    )
    re0, im0 = full[:BLOCK], full[BLOCK:]
    top = lax.broadcasted_iota(jnp.int32, re0.shape, 0) == 0
    spec[0] = re0
    spec[1] = jnp.where(top, 0.0, im0)
    spec[2] = jnp.where(top, im0, re0)
    hb = POINTS // 2

    def filter_block(b, carry):
        start = pl.multiple_of(b * BLOCK, BLOCK)
        window = inner[pl.ds(start, 2 * BLOCK), :]
        mine = seg[pl.ds(pl.multiple_of(start + 16 + BLOCK, 16), BLOCK), :]
        mine = jnp.concatenate([mine] * (POINTS // 128), axis=1)
        ids = lines[pl.ds(b, 1), :]

        def one(s, acc):
            f = jnp.where(ids == s, fwd[...], 0.0).astype(jnp.bfloat16)
            w = jnp.where(mine == s, back[...], 0.0).astype(jnp.bfloat16)
            z = jnp.dot(f, window, preferred_element_type=jnp.float32)
            a, bb = z[:hb], z[hb:]
            re = a * spec[0] - bb * spec[1]
            im = a * spec[1] + bb * spec[2]
            prod = jnp.concatenate([re, im], axis=0).astype(jnp.bfloat16)
            return acc + jnp.dot(w, prod, preferred_element_type=jnp.float32)

        conv = lax.fori_loop(bounds[b], bounds[blocks + b] + 1, one, jnp.zeros((BLOCK, out.shape[1]), jnp.float32))
        here = pl.ds(pl.multiple_of(start + BLOCK, BLOCK), BLOCK)
        mixed = gate[here, :] * (conv + skip[...] * window[BLOCK:].astype(jnp.float32))
        out[pl.ds(start, BLOCK), :] = mixed.astype(jnp.bfloat16)
        return carry

    lax.fori_loop(0, blocks - 1, filter_block, 0)


def filter_gate(inner, gate, filt, skip, seg, lines, bounds, wave, fwd, back):
    ext, wide = inner.shape
    rows = ext - BLOCK
    cols = min(512, wide)
    column = lambda n: pl.BlockSpec((n, cols), lambda j, b: (0, j))
    whole = lambda v: pl.BlockSpec(v.shape, lambda j, b: (0,) * v.ndim)
    return pl.pallas_call(
        conv_kernel,
        grid_spec=pltpu.PrefetchScalarGridSpec(
            num_scalar_prefetch=1,
            grid=(wide // cols,),
            in_specs=[
                column(ext),
                column(ext),
                pl.BlockSpec((cols, filt.shape[1]), lambda j, b: (j, 0)),
                column(1),
                whole(seg),
                whole(lines),
                whole(wave),
                whole(fwd),
                whole(back),
            ],
            out_specs=column(rows),
            scratch_shapes=[pltpu.VMEM((3, BLOCK, cols), jnp.float32)],
        ),
        out_shape=jax.ShapeDtypeStruct((rows, wide), jnp.bfloat16),
        compiler_params=pltpu.CompilerParams(vmem_limit_bytes=40 << 20),
        name="filter_gate",
    )(bounds, inner, gate, filt, skip, seg, lines, wave, fwd, back)


def distances(segment_ids):
    count = segment_ids.shape[0]
    places = jnp.arange(count, dtype=jnp.int32)
    earlier = jnp.concatenate([segment_ids[:1] - 1, segment_ids[:-1]])
    starts = jnp.where(segment_ids != earlier, places, jnp.zeros_like(places))
    return places - lax.cummax(starts, axis=0)


def per_device(nt, nc, tokens, norm_gain, in_weight, short_taps, long_filter, skip_bias, segment_ids):
    rows = tokens.shape[0]
    first = lax.axis_index("context") * rows
    pad = jnp.full((HALO,), -1, jnp.int32)
    ids = lax.dynamic_slice_in_dim(jnp.concatenate([pad, segment_ids]), first, rows + HALO, 0)
    dist = lax.dynamic_slice_in_dim(jnp.concatenate([pad, distances(segment_ids)]), first, rows + HALO, 0)
    bounds = jnp.concatenate([ids[HALO::BLOCK], ids[HALO + BLOCK - 1 :: BLOCK]])
    spread = lambda v: jnp.broadcast_to(v[:, None], (rows + HALO, 128))
    forward, back = transforms()
    near = lambda v: jnp.asarray(v.astype(jnp.bfloat16).astype(np.float32))
    last = jnp.zeros((1,), jnp.int32)
    n = rows // BLOCK
    bounds = jnp.concatenate([bounds[:n], last, bounds[n:]])
    lines = jnp.stack([ids[16 + b * BLOCK : 16 + (b + 2) * BLOCK] for b in range(n)])
    inner, gate = project_all(nt, nc, tokens, in_weight, norm_gain[None, :], short_taps, spread(dist))
    return filter_gate(
        inner, gate, long_filter, skip_bias[None, :], spread(ids), lines, bounds,
        jnp.asarray(forward[:, : long_filter.shape[1]]), near(forward), near(back),
    )


def solution(mesh):
    placed = (
        P(("dp", "context"), "tensor"),
        P(),
        P(None, "context", "tensor"),
        P(None, None, "tensor"),
        P("tensor", None),
        P("tensor"),
        P("dp"),
    )
    return jax.shard_map(
        functools.partial(per_device, mesh.shape["tensor"], mesh.shape["context"]),
        mesh=mesh,
        in_specs=placed,
        out_specs=P(("dp", "context"), "tensor"),
        check_vma=False,
    )
```

```python
import functools
import math

import jax
import jax.numpy as jnp
import numpy as np
from jax import lax
from jax.experimental import pallas as pl
from jax.experimental.pallas import tpu as pltpu
from jax.sharding import PartitionSpec as P

MESH = pl.DeviceIdType.MESH
PIECES = 8
HALO = 144
BLOCK = 128
POINTS = 256
PARTS = 6


def gather_kernel(nt, nc, x_in, w_in, gain, taps, dist, inner, gate, xbuf, wbuf, normed, out, strip, loc, xs, xr, ys, yr, ps, pr, cs, cr, os_, or_, hs, hr):
    d = lax.axis_index("dp")
    i = lax.axis_index("context")
    t = lax.axis_index("tensor")
    y, c = i // 2, i % 2
    ny = nc // 2
    rows = x_in.shape[0] // PIECES
    deep = w_in.shape[1]
    half = deep // 2
    sib = (d, i + 1 - 2 * c, t)
    peer = (1 - d, i, t)

    mine_x = pltpu.make_async_copy(x_in, xbuf.at[t], loc.at[0])
    mine_w = pltpu.make_async_copy(w_in, wbuf.at[:, pl.ds(i * deep, deep), :], loc.at[1])
    mine_x.start()
    mine_w.start()

    bar = pltpu.get_barrier_semaphore()

    def greet(dev):
        pl.semaphore_signal(bar, inc=1, device_id=dev, device_id_type=MESH)

    greet(sib)
    greet(peer)
    peers = jnp.int32(2)
    for cond, dev in (
        (t > 0, (d, i, t - 1)),
        (t < nt - 1, (d, i, t + 1)),
        (y > 0, (d, i - 2, t)),
        (y < ny - 1, (d, i + 2, t)),
        ((c == 0) & (i > 0), (d, i - 1, t)),
        ((c == 1) & (i < nc - 1), (d, i + 1, t)),
    ):
        peers = peers + cond.astype(jnp.int32)

        @pl.when(cond)
        def _():
            greet(dev)

    pl.semaphore_wait(bar, peers)

    def spot(r):
        return pl.multiple_of(lax.rem(r + PIECES - 2, PIECES) * rows, rows)

    def xcopy(side, hop, r, block, first):
        place = pl.ds(spot(r), rows)
        dst = xbuf.at[block, place, :]
        src = x_in.at[place, :] if first else dst
        to = (d, i, t + 1) if side == 0 else (d, i, t - 1)
        return pltpu.make_async_remote_copy(src, dst, xs.at[side, hop, r], xr.at[side, hop, r], device_id=to, device_id_type=MESH)

    def x_sends(side, hop):
        return (t < nt - 1) & (t - hop >= 0) if side == 0 else (t > 0) & (t + hop < nt)

    def x_takes(side, hop):
        return t - 1 - hop >= 0 if side == 0 else t + 1 + hop < nt

    def x_sent(side, hop):
        return t - hop if side == 0 else t + hop

    def x_taken(side, hop):
        return t - 1 - hop if side == 0 else t + 1 + hop

    def when(cond, f):
        pl.when(cond)(f)

    def branch(g):
        span = w_in.shape[2] // (PARTS // 3)
        return g // (PARTS // 3), pl.ds(g % (PARTS // 3) * span, span)

    def wspan(block, part):
        return pl.ds(pl.multiple_of(block * deep + part * half, half), half)

    def ycopy(side, hop, g, yb, first):
        place = wspan(yb * 2 + c, d)
        n, cols = branch(g)
        dst = wbuf.at[n, place, cols]
        src = w_in.at[n, pl.ds(pl.multiple_of(d * half, half), half), cols] if first else dst
        to = (d, i + 2, t) if side == 0 else (d, i - 2, t)
        return pltpu.make_async_remote_copy(src, dst, ys.at[side, hop, g], yr.at[side, hop, g], device_id=to, device_id_type=MESH)

    def y_sends(side, hop):
        return (y < ny - 1) & (y - hop >= 0) if side == 0 else (y > 0) & (y + hop < ny)

    def y_takes(side, hop):
        return y - 1 - hop >= 0 if side == 0 else y + 1 + hop < ny

    def y_sent(side, hop):
        return y - hop if side == 0 else y + hop

    def y_taken(side, hop):
        return y - 1 - hop if side == 0 else y + 1 + hop

    def pcopy(side, hop, g, yb, part):
        n, cols = branch(g)
        at = wbuf.at[n, wspan(yb * 2 + c, part), cols]
        return pltpu.make_async_remote_copy(at, at, ps.at[side, hop, g], pr.at[side, hop, g], device_id=peer, device_id_type=MESH)

    def ccopy(side, hop, g, via, yb, core, part):
        n, cols = branch(g)
        at = wbuf.at[n, wspan(yb * 2 + core, part), cols]
        return pltpu.make_async_remote_copy(at, at, cs.at[side, hop, g, via], cr.at[side, hop, g, via], device_id=sib, device_id_type=MESH)

    def ocopy(block):
        at = wbuf.at[:, pl.ds(pl.multiple_of(block * deep, deep), deep), :]
        return pltpu.make_async_remote_copy(w_in, at, os_, or_, device_id=sib, device_id_type=MESH)

    sides = (0, 1)

    for g in range(PARTS):
        for side in sides:
            when(y_sends(side, 0), lambda: ycopy(side, 0, g, y, True).start())

    def start_own(r, carry):
        for side in sides:
            when(x_sends(side, 0), lambda: xcopy(side, 0, r, t, True).start())
        return carry

    lax.fori_loop(0, PIECES, start_own, 0)
    ocopy(i).start()

    def pass_x(step, carry):
        hop, r = step // PIECES, step % PIECES
        for side in sides:
            @pl.when(x_takes(side, hop))
            def _():
                xcopy(side, hop, r, x_taken(side, hop), False).wait_recv()

            when(x_sends(side, hop + 1), lambda: xcopy(side, hop + 1, r, x_sent(side, hop + 1), False).start())
        return carry

    def pass_w(g):
        for hop in range(ny - 1):
            for side in sides:
                @pl.when(y_takes(side, hop))
                def _():
                    yb = y_taken(side, hop)
                    ycopy(side, hop, g, yb, False).wait_recv()
                    pcopy(side, hop, g, yb, d).start()
                    ccopy(side, hop, g, 0, yb, c, d).start()

                if hop + 1 < ny - 1:
                    when(y_sends(side, hop + 1), lambda: ycopy(side, hop + 1, g, y_sent(side, hop + 1), False).start())

    def pass_p(g):
        for hop in range(ny - 1):
            for side in sides:
                @pl.when(y_takes(side, hop))
                def _():
                    yb = y_taken(side, hop)
                    pcopy(side, hop, g, yb, 1 - d).wait_recv()
                    ccopy(side, hop, g, 1, yb, c, 1 - d).start()

    steps = (nt - 2) * PIECES
    cuts = [1 + (g + 1) * steps // (PARTS + 2) for g in range(PARTS)]
    at = 0
    for g in range(PARTS):
        lax.fori_loop(at, cuts[g], pass_x, 0)
        at = cuts[g]
        pass_w(g)
        if g:
            pass_p(g - 1)
    lax.fori_loop(at, steps, pass_x, 0)
    pass_p(PARTS - 1)

    mine_x.wait()
    mine_w.wait()
    ocopy(sib[1]).wait_recv()
    for g in range(PARTS):
        for hop in range(ny - 1):
            for side in sides:
                @pl.when(y_takes(side, hop))
                def _():
                    yb = y_taken(side, hop)
                    ccopy(side, hop, g, 0, yb, 1 - c, d).wait_recv()
                    ccopy(side, hop, g, 1, yb, 1 - c, 1 - d).wait_recv()

    wide = w_in.shape[2]
    tile = min(512, wide)
    feats = x_in.shape[1]

    def project(r):
        for side in sides:
            when(x_takes(side, nt - 2), lambda: xcopy(side, nt - 2, r, x_taken(side, nt - 2), False).wait_recv())
        place = pl.ds(spot(r), rows)
        total = jnp.zeros((rows, 1), jnp.float32)
        for k in range(nt):
            v = xbuf[k, place, :].astype(jnp.float32)
            total = total + jnp.sum(v * v, axis=1, keepdims=True)
        scale = lax.rsqrt(total * (1.0 / (feats * nt)) + 1e-06)
        for k in range(nt):
            v = xbuf[k, place, :].astype(jnp.float32)
            cols = pl.ds(k * feats, feats)
            normed[:, cols] = (v * scale * gain[:, cols]).astype(jnp.bfloat16)
        to = pl.ds(pl.multiple_of(HALO + spot(r), 16), rows)

        def one(n, carry):
            g = n // (wide // tile)
            cols = pl.ds(pl.multiple_of((n % (wide // tile)) * tile, tile), tile)
            out[g, to, cols] = jnp.dot(normed[...], wbuf[g, :, cols], preferred_element_type=jnp.float32).astype(jnp.bfloat16)
            return carry

        lax.fori_loop(0, 3 * (wide // tile), one, 0)

    ntaps = taps.shape[1]

    def featurize(start):
        start = pl.multiple_of(start, BLOCK)
        at = pl.ds(start, BLOCK)

        def column(n, carry):
            cols = pl.ds(pl.multiple_of(n * 128, 128), 128)
            near = dist[pl.ds(pl.multiple_of(start + 16, 16), BLOCK), :]
            sums = [None] * 3
            for g in range(3):
                strip[g] = out[g, pl.ds(start, BLOCK + 16), cols].astype(jnp.float32)
            for lag in range(ntaps):
                valid = near >= lag
                for g in range(3):
                    term = taps[g, lag : lag + 1, cols] * strip[g, 16 - lag : 16 - lag + BLOCK, :]
                    term = jnp.where(valid, term, 0.0)
                    sums[g] = term if lag == 0 else sums[g] + term
            inner[at, cols] = (sums[1] * sums[2]).astype(jnp.bfloat16)
            gate[at, cols] = sums[0]
            return carry

        lax.fori_loop(0, wide // 128, column, 0)

    def project_step(r, carry):
        project(r)
        return carry

    def both(r, carry):
        project(r)
        featurize(BLOCK + spot(r))
        return carry

    total_rows = rows * PIECES

    def hcopy():
        return pltpu.make_async_remote_copy(
            out.at[:, pl.ds(total_rows, HALO), :], out.at[:, pl.ds(0, HALO), :], hs, hr, device_id=(d, i + 1, t), device_id_type=MESH
        )

    @pl.when(i == 0)
    def _():
        out[:, 0:HALO, :] = jnp.zeros((3, HALO, wide), jnp.bfloat16)

    lax.fori_loop(0, 2, project_step, 0)
    when(i < nc - 1, lambda: hcopy().start())
    featurize(BLOCK + (PIECES - 1) * rows)
    lax.fori_loop(2, 4, project_step, 0)
    when(i > 0, lambda: hcopy().wait_recv())
    featurize(0)
    featurize(BLOCK)
    featurize(BLOCK + rows)
    lax.fori_loop(4, PIECES, both, 0)
    featurize(BLOCK + (PIECES - 2) * rows)

    def drain(r, carry):
        for hop in range(nt - 1):
            for side in sides:
                when(x_sends(side, hop), lambda: xcopy(side, hop, r, x_sent(side, hop), False).wait_send())
        return carry

    lax.fori_loop(0, PIECES, drain, 0)
    for g in range(PARTS):
        for hop in range(ny - 1):
            for side in sides:
                when(y_sends(side, hop), lambda: ycopy(side, hop, g, y_sent(side, hop), False).wait_send())

                @pl.when(y_takes(side, hop))
                def _():
                    yb = y_taken(side, hop)
                    pcopy(side, hop, g, yb, d).wait_send()
                    ccopy(side, hop, g, 0, yb, c, d).wait_send()
                    ccopy(side, hop, g, 1, yb, c, 1 - d).wait_send()
    ocopy(i).wait_send()
    when(i < nc - 1, lambda: hcopy().wait_send())


def project_all(nt, nc, tokens, in_weight, gain, taps, dist):
    rows, feats = tokens.shape
    deep, wide = in_weight.shape[1:]
    ny = nc // 2
    dma = pltpu.SemaphoreType.DMA
    hops = max(ny - 1, 1)
    return pl.pallas_call(
        functools.partial(gather_kernel, nt, nc),
        out_shape=(
            jax.ShapeDtypeStruct((BLOCK + rows, wide), jnp.bfloat16),
            jax.ShapeDtypeStruct((BLOCK + rows, wide), jnp.float32),
        ),
        in_specs=[pl.BlockSpec(memory_space=pl.ANY)] * 2 + [pl.BlockSpec(memory_space=pltpu.VMEM)] * 3,
        out_specs=(pl.BlockSpec(memory_space=pltpu.VMEM),) * 2,
        scratch_shapes=[
            pltpu.VMEM((nt, rows, feats), jnp.bfloat16),
            pltpu.VMEM((3, nc * deep, wide), jnp.bfloat16),
            pltpu.VMEM((rows // PIECES, nt * feats), jnp.bfloat16),
            pltpu.VMEM((3, HALO + rows, wide), jnp.bfloat16),
            pltpu.VMEM((3, BLOCK + 16, 128), jnp.float32),
            dma((2,)),
            dma((2, nt - 1, PIECES)),
            dma((2, nt - 1, PIECES)),
            dma((2, hops, PARTS)),
            dma((2, hops, PARTS)),
            dma((2, hops, PARTS)),
            dma((2, hops, PARTS)),
            dma((2, hops, PARTS, 2)),
            dma((2, hops, PARTS, 2)),
            dma,
            dma,
            dma,
            dma,
        ],
        compiler_params=pltpu.CompilerParams(collective_id=0, has_side_effects=True, vmem_limit_bytes=56 << 20),
        name="gather_project",
    )(tokens, in_weight, gain, taps, dist)


def transforms():
    k = np.arange(POINTS // 2)[:, None]
    n = np.arange(POINTS)[None, :]
    angle = 2 * np.pi * ((k * n) % POINTS) / POINTS
    cos, sin = np.cos(angle), -np.sin(angle)
    sin[0] = np.where(np.arange(POINTS) % 2 == 0, 1.0, -1.0)
    forward = np.concatenate([cos, sin], axis=0)
    weight = np.full((POINTS, 1), 2.0 / POINTS)
    weight[0] = weight[POINTS // 2] = 1.0 / POINTS
    back = (forward * weight).T[BLOCK:]
    return forward.astype(np.float32), back.astype(np.float32)


def conv_kernel(bounds, inner, gate, filt, skip, seg, wave, fwd, back, out, spec):
    blocks = inner.shape[0] // BLOCK
    wide = out.shape[1]
    full = lax.dot_general(
        wave[...], filt[...], (((1,), (1,)), ((), ())), precision=lax.Precision.HIGHEST, preferred_element_type=jnp.float32
    )
    re0, im0 = full[:BLOCK], full[BLOCK:]
    top = lax.broadcasted_iota(jnp.int32, re0.shape, 0) == 0
    spec[0] = re0
    spec[1] = jnp.where(top, 0.0, im0)
    spec[2] = jnp.where(top, im0, re0)
    f = fwd[...]
    w = back[...]
    hb = POINTS // 2

    def filter_block(b, carry):
        start = pl.multiple_of(b * BLOCK, BLOCK)
        window = inner[pl.ds(start, 2 * BLOCK), :].astype(jnp.float32)
        ids = seg[pl.ds(pl.multiple_of(start + 16, 16), 2 * BLOCK), :]
        ids = jnp.concatenate([ids] * (wide // 128), axis=1)
        mine = ids[BLOCK:]

        def one(s, acc):
            x = jnp.where(ids == s, window, 0.0).astype(jnp.bfloat16)
            z = jnp.dot(f, x, preferred_element_type=jnp.float32)
            a, bb = z[:hb], z[hb:]
            re = a * spec[0] - bb * spec[1]
            im = a * spec[1] + bb * spec[2]
            prod = jnp.concatenate([re, im], axis=0).astype(jnp.bfloat16)
            return jnp.where(mine == s, jnp.dot(w, prod, preferred_element_type=jnp.float32), acc)

        conv = lax.fori_loop(bounds[b], bounds[blocks + b] + 1, one, jnp.zeros((BLOCK, out.shape[1]), jnp.float32))
        here = pl.ds(pl.multiple_of(start + BLOCK, BLOCK), BLOCK)
        mixed = gate[here, :] * (conv + skip[...] * window[BLOCK:])
        out[pl.ds(start, BLOCK), :] = mixed.astype(jnp.bfloat16)
        return carry

    lax.fori_loop(0, blocks - 1, filter_block, 0)


def filter_gate(inner, gate, filt, skip, seg, bounds, wave, fwd, back):
    ext, wide = inner.shape
    rows = ext - BLOCK
    cols = min(512, wide)
    column = lambda n: pl.BlockSpec((n, cols), lambda j, b: (0, j))
    whole = lambda v: pl.BlockSpec(v.shape, lambda j, b: (0,) * v.ndim)
    return pl.pallas_call(
        conv_kernel,
        grid_spec=pltpu.PrefetchScalarGridSpec(
            num_scalar_prefetch=1,
            grid=(wide // cols,),
            in_specs=[
                column(ext),
                column(ext),
                pl.BlockSpec((cols, filt.shape[1]), lambda j, b: (j, 0)),
                column(1),
                whole(seg),
                whole(wave),
                whole(fwd),
                whole(back),
            ],
            out_specs=column(rows),
            scratch_shapes=[pltpu.VMEM((3, BLOCK, cols), jnp.float32)],
        ),
        out_shape=jax.ShapeDtypeStruct((rows, wide), jnp.bfloat16),
        compiler_params=pltpu.CompilerParams(vmem_limit_bytes=60 << 20),
        name="filter_gate",
    )(bounds, inner, gate, filt, skip, seg, wave, fwd, back)


def distances(segment_ids):
    count = segment_ids.shape[0]
    places = jnp.arange(count, dtype=jnp.int32)
    earlier = jnp.concatenate([segment_ids[:1] - 1, segment_ids[:-1]])
    starts = jnp.where(segment_ids != earlier, places, jnp.zeros_like(places))
    return places - lax.cummax(starts, axis=0)


def per_device(nt, nc, tokens, norm_gain, in_weight, short_taps, long_filter, skip_bias, segment_ids):
    rows = tokens.shape[0]
    first = lax.axis_index("context") * rows
    pad = jnp.full((HALO,), -1, jnp.int32)
    ids = lax.dynamic_slice_in_dim(jnp.concatenate([pad, segment_ids]), first, rows + HALO, 0)
    dist = lax.dynamic_slice_in_dim(jnp.concatenate([pad, distances(segment_ids)]), first, rows + HALO, 0)
    bounds = jnp.concatenate([ids[HALO::BLOCK], ids[HALO + BLOCK - 1 :: BLOCK]])
    spread = lambda v: jnp.broadcast_to(v[:, None], (rows + HALO, 128))
    forward, back = transforms()
    last = jnp.zeros((1,), jnp.int32)
    n = rows // BLOCK
    bounds = jnp.concatenate([bounds[:n], last, bounds[n:]])
    inner, gate = project_all(nt, nc, tokens, in_weight, norm_gain[None, :], short_taps, spread(dist))
    return filter_gate(
        inner, gate, long_filter, skip_bias[None, :], spread(ids), bounds,
        jnp.asarray(forward[:, : long_filter.shape[1]]), jnp.asarray(forward, jnp.bfloat16), jnp.asarray(back, jnp.bfloat16),
    )


def solution(mesh):
    placed = (
        P(("dp", "context"), "tensor"),
        P(),
        P(None, "context", "tensor"),
        P(None, None, "tensor"),
        P("tensor", None),
        P("tensor"),
        P("dp"),
    )
    return jax.shard_map(
        functools.partial(per_device, mesh.shape["tensor"], mesh.shape["context"]),
        mesh=mesh,
        in_specs=placed,
        out_specs=P(("dp", "context"), "tensor"),
        check_vma=False,
    )
```
